256 devices in a mesh: chan: 32 (over y, z_lo, core), win: 8 (over x, z_hi).
Axes of the slice: x: 4, y: 4, z: 8 (z_hi: 2, z_lo: 4; z = z_hi * 4 + z_lo), core: 2. Of those that a mesh axis runs over, the one named last changes fastest.
Arguments:
- record: float32 [4096, 12288], P('chan', 'win')
- owners: int32 [3], replicated, may hold values from 0 to 31, as said below
- pair_mask: int32 [32, 32], replicated, may hold values from 0 to 1, as said below
Outputs:
- correlations: float32 [3, 81, 128, 4096], P(None, None, 'win', 'chan')
The draws below stay inside these ranges and needn't reach their ends.
Inputs may be any that keep to these rules, and one draw needn't show every extreme that they name: `owners`: 3 different channel blocks. pair_mask[o, b] is 0 wherever b < o.
All inputs are finite; a program needn't handle non-finite values.
Results may differ from the reference program's by a relative error of at most 0.0041.
Values may be sent and summed in bfloat16 or wider, within the bound.
No kernel may reach another device: no remote copies, remote signals or barrier semaphores. Data moves between devices by JAX's collectives and lax.ppermute only.
A program may use at most 128 MiB of HBM per device.

```python
import jax
import jax.numpy as jnp
from jax import lax

CH_DEV = 128
LAG = 40
STEPS = 3
BLOCKS = 32
CHANNELS = 4096
TIME = 12288


def draw_record(key, part):
    key = jax.random.fold_in(key, 11)
    key_gain, key_env, key_noise, key_common = jax.random.split(key, 4)
    chan_pos = jnp.arange(CHANNELS, dtype=jnp.float32) / max(CHANNELS - 1, 1)
    time_pos = jnp.arange(TIME, dtype=jnp.float32) / max(TIME - 1, 1)
    gain = 3.0 ** chan_pos * jnp.exp(jax.random.uniform(key_gain, (CHANNELS,), jnp.float32, -0.35, 0.35))
    envelope = 3.0 ** time_pos * jnp.exp(jax.random.uniform(key_env, (TIME,), jnp.float32, -0.35, 0.35))
    noise = jax.random.normal(key_noise, (CHANNELS, TIME), jnp.float32)
    shared = 0.5
    common = shared * jax.random.normal(key_common, (TIME,), jnp.float32) * envelope
    return gain[:, None] * envelope[None, :] * noise + common[None, :]


def draw_owners(key, part):
    key = jax.random.fold_in(key, 12)
    key_middle, key_order = jax.random.split(key, 2)
    middle = jax.random.permutation(key_middle, BLOCKS - 2).astype(jnp.int32) + 1
    picks = jnp.concatenate([jnp.zeros((1,), jnp.int32), middle[:STEPS - 2], jnp.full((1,), BLOCKS - 1, jnp.int32)])
    order = jax.random.permutation(key_order, STEPS)
    return picks[order].astype(jnp.int32)


def draw_pair_mask(key, part):
    key = jax.random.fold_in(key, 13)
    index = jnp.arange(BLOCKS, dtype=jnp.int32)
    upper = index[:, None] <= index[None, :]
    chosen = jax.random.randint(key, (BLOCKS, BLOCKS), 0, 4) > 0
    return jnp.logical_and(upper, chosen).astype(jnp.int32)


def setup_inputs(seed: int = 0) -> dict:
    key_of = jax.random.split(jax.random.key(seed), 4)
    record = draw_record(jax.random.fold_in(key_of[3], 71), 0)
    owners = draw_owners(jax.random.fold_in(key_of[3], 71), 0)
    pair_mask = draw_pair_mask(jax.random.fold_in(key_of[3], 71), 0)
    return dict(record=record, owners=owners, pair_mask=pair_mask)


def reference(record, owners, pair_mask):
    common = lax.optimization_barrier(jnp.mean(record, axis=0))
    cleaned = record - common[None, :]
    power = lax.optimization_barrier(jnp.mean(cleaned * cleaned, axis=1))
    whitened = (cleaned / jnp.sqrt(power + 1e-06)[:, None]).astype(jnp.bfloat16)
    wide = whitened.astype(jnp.float32)
    norm_scale = 1.0 / jnp.sqrt(jnp.float32(TIME))
    lag_count = 2 * LAG + 1
    results = []
    for step_index in range(STEPS):
        owner_id = owners[step_index].astype(jnp.int32)
        source = lax.dynamic_slice_in_dim(wide, owner_id * CH_DEV, CH_DEV, 0)
        source_pad = jnp.pad(source, ((0, 0), (LAG, LAG)))

        def one_lag(lag_index):
            start = (2 * LAG - lag_index).astype(jnp.int32)
            shifted = lax.dynamic_slice_in_dim(source_pad, start, TIME, 1)
            return lax.dot_general(shifted, wide, (((1,), (1,)), ((), ())), precision=lax.Precision.HIGHEST, preferred_element_type=jnp.float32)
        lagged = lax.map(one_lag, jnp.arange(lag_count, dtype=jnp.int32))
        block_flags = pair_mask[owner_id].astype(jnp.float32)
        column_flags = jnp.repeat(block_flags, CH_DEV)
        results.append(lagged * column_flags[None, None, :] * norm_scale)
    return jnp.stack(results)
```

```python
import functools
import math

import jax
import jax.numpy as jnp
from jax import lax
from jax.experimental import pallas as pl
from jax.experimental.pallas import tpu as pltpu
from jax.sharding import PartitionSpec as P

LAG = 40
STEPS = 3
LAGS = 2 * LAG + 1
HALF = LAG + 1
EDGE = 128


def permute(value, axis, target):
    size = lax.axis_size(axis)
    return lax.ppermute(value, axis, [(i, target(i)) for i in range(size)])


def core_flip(i):
    return i ^ 1


def z_shift(d):
    return lambda i: (i & ~6) | ((((i >> 1) + d) & 3) << 1)


def y_shift(d):
    return lambda i: (i & 7) | ((((i >> 3) + d) & 3) << 3)


def hi_flip(i):
    return i ^ 1


def x_shift(d):
    return lambda i: (i & 1) | ((((i >> 1) + d) & 3) << 1)


def correlate_kernel(index_ref, *refs, span, chunk, group):
    own_refs, block_refs = refs[:4], refs[4:12]
    out_ref, own, block, left, right, total = refs[12:]
    rows = own.shape[0]
    share = rows // STEPS
    width = block.shape[0]
    length = block.shape[1] - EDGE
    quarter = span // 4
    bf16 = jnp.bfloat16

    own[:, :EDGE] = jnp.zeros((rows, EDGE), bf16)
    own[:, EDGE + length:] = jnp.zeros((rows, EDGE), bf16)
    block[:, length:] = jnp.zeros((width, EDGE), bf16)
    own_power = jnp.zeros((rows, EDGE), jnp.float32)
    for d in range(4):
        where = index_ref[d]
        for w in range(length // span):
            piece = own_refs[d][:, w * quarter:(w + 1) * quarter]
            start = pl.multiple_of(EDGE + w * span + where * quarter, EDGE)
            own[:, pl.ds(start, quarter)] = piece
            wide = piece.astype(jnp.float32)
            for k in range(quarter // EDGE):
                part = wide[:, k * EDGE:(k + 1) * EDGE]
                own_power += part * part
    block_power = jnp.zeros((width, EDGE), jnp.float32)
    for d in range(8):
        piece = block_refs[d][...]
        start = pl.multiple_of(index_ref[4 + d] * span, EDGE)
        block[:, pl.ds(start, span)] = piece
        wide = piece.astype(jnp.float32)
        for k in range(span // EDGE):
            part = wide[:, k * EDGE:(k + 1) * EDGE]
            block_power += part * part
    own_power = jnp.sum(own_power, axis=1, keepdims=True) / length
    block_power = jnp.sum(block_power, axis=1, keepdims=True) / length
    own_scale = 1.0 / jnp.sqrt(own_power + 1e-06)
    block_scale = 1.0 / jnp.sqrt(block_power + 1e-06)
    block_scale = jnp.transpose(jnp.broadcast_to(block_scale, (width, width)))[:1]

    def product(a, b):
        return lax.dot_general(a, b, (((1,), (1,)), ((), ())), preferred_element_type=jnp.float32)

    lead = own[:, :2 * EDGE]
    for l in range(HALF):
        left[l * rows:(l + 1) * rows, :EDGE] = lead[:, LAG - l:LAG - l + EDGE]
    before = jnp.concatenate([jnp.zeros((width, EDGE - HALF), bf16), block[:, :HALF]], axis=1)
    total[:, :width] = jnp.zeros((HALF * rows, width), jnp.float32)
    total[:, width:] = product(left[:, :EDGE], before)

    def step(k, carry):
        start = pl.multiple_of(k * chunk, EDGE)
        mine = own[:, pl.ds(start + EDGE, chunk + EDGE)]
        theirs = block[:, pl.ds(start, chunk + EDGE)]
        right[:width] = theirs[:, :chunk]
        right[width:] = theirs[:, HALF:HALF + chunk]
        for g in range(0, HALF, group):
            stop = min(g + group, HALF)
            for l in range(g, stop):
                left[l * rows:(l + 1) * rows] = mine[:, LAG - l:LAG - l + chunk]
            part = slice(g * rows, stop * rows)
            total[part] += product(left[part], right[...])
        return carry

    lax.fori_loop(0, length // chunk, step, 0)
    norm = 1.0 / math.sqrt(length)
    for s in range(STEPS):
        flag = index_ref[12 + s].astype(jnp.float32) * norm
        scale = own_scale[s * share:(s + 1) * share] * (block_scale * flag)
        for l in range(HALF):
            at = slice(l * rows + s * share, l * rows + (s + 1) * share)
            out_ref[s, l] = total[at, :width] * scale
            if l + HALF < LAGS:
                out_ref[s, l + HALF] = total[at, width:] * scale


def correlate(index, own, block):
    rows, width, span = own[0].shape[0], block[0].shape[0], block[0].shape[1]
    length = span * len(block)
    chunk = 3072
    vmem = pl.BlockSpec(memory_space=pltpu.VMEM)
    return pl.pallas_call(
        functools.partial(correlate_kernel, span=span, chunk=chunk, group=14),
        out_shape=jax.ShapeDtypeStruct((STEPS, LAGS, rows // STEPS, width), jnp.float32),
        in_specs=[pl.BlockSpec(memory_space=pltpu.SMEM)] + [vmem] * 12,
        out_specs=vmem,
        scratch_shapes=[
            pltpu.VMEM((rows, length + 2 * EDGE), jnp.bfloat16),
            pltpu.VMEM((width, length + EDGE), jnp.bfloat16),
            pltpu.VMEM((HALF * rows, chunk), jnp.bfloat16),
            pltpu.VMEM((2 * width, chunk), jnp.bfloat16),
            pltpu.VMEM((HALF * rows, 2 * width), jnp.float32),
        ],
        compiler_params=pltpu.CompilerParams(vmem_limit_bytes=56 * 2**20),
        cost_estimate=pl.CostEstimate(
            flops=2 * HALF * rows * 2 * width * length, bytes_accessed=6 * 2**20, transcendentals=0
        ),
    )(index, *own, *block)


def local(record, owners, pair_mask):
    width, span = record.shape
    channels = width * lax.axis_size("chan")
    chan, win = lax.axis_index("chan"), lax.axis_index("win")

    sums = jnp.sum(record, axis=0)
    sums = sums + permute(sums, "chan", core_flip)
    sums = sums + (permute(sums, "chan", z_shift(1)) + permute(sums, "chan", z_shift(2)) + permute(sums, "chan", z_shift(3)))
    sums = sums + (permute(sums, "chan", y_shift(1)) + permute(sums, "chan", y_shift(2)) + permute(sums, "chan", y_shift(3)))
    cleaned = (record - (sums / channels)[None, :]).astype(jnp.bfloat16)

    far = permute(cleaned, "win", hi_flip)
    block = [cleaned] + [permute(cleaned, "win", x_shift(d)) for d in (1, 2, 3)]
    block += [far] + [permute(far, "win", x_shift(d)) for d in (1, 2, 3)]

    quarter = span // 4
    pieces = cleaned.reshape(8, 8, 2, 4, quarter).transpose(3, 1, 0, 2, 4).reshape(256, 2, quarter)
    pieces = lax.all_to_all(pieces, ("chan", "win"), 0, 0).reshape(32, 8, 2, quarter)
    mine = jnp.stack([lax.dynamic_index_in_dim(pieces, owners[s], 0, False) for s in range(STEPS)])
    pair = jnp.stack([mine, permute(mine, "chan", core_flip)])
    core = chan & 1
    pair = jnp.where(core == 0, pair, pair[::-1])
    lo = (chan >> 1) & 3
    ring = [pair] + [permute(pair, "chan", z_shift(d)) for d in (1, 2, 3)]
    ring = jnp.stack(ring + ring)
    ring = lax.dynamic_slice_in_dim(ring[::-1], 3 - lo, 4, 0)
    ring = ring.reshape(8, STEPS, 8, 2, quarter).transpose(1, 0, 3, 2, 4).reshape(STEPS * 16, 8 * quarter)
    own = [ring] + [permute(ring, "chan", y_shift(d)) for d in (1, 2, 3)]

    y, x, hi = chan >> 3, win >> 1, win & 1
    index = [(y - d) & 3 for d in range(4)]
    index += [(((x - d) & 3) << 1) | hi for d in range(4)] + [(((x - d) & 3) << 1) | (1 - hi) for d in range(4)]
    index += [pair_mask[owners[s], chan] for s in range(STEPS)]
    index = jnp.stack(index).astype(jnp.int32)
    return correlate(index, own, block)


def solution(mesh):
    in_specs = (P("chan", "win"), P(), P())
    out_specs = P(None, None, "win", "chan")
    return jax.shard_map(local, mesh=mesh, in_specs=in_specs, out_specs=out_specs, check_vma=False)
```

```python
import functools
import math

import jax
import jax.numpy as jnp
from jax import lax
from jax.experimental import pallas as pl
from jax.experimental.pallas import tpu as pltpu
from jax.sharding import PartitionSpec as P

LAG = 40
STEPS = 3
LAGS = 2 * LAG + 1
HALF = LAG + 1
EDGE = 128


def permute(value, axis, target):
    size = lax.axis_size(axis)
    return lax.ppermute(value, axis, [(i, target(i)) for i in range(size)])


def core_flip(i):
    return i ^ 1


def z_shift(d):
    return lambda i: (i & ~6) | ((((i >> 1) + d) & 3) << 1)


def y_shift(d):
    return lambda i: (i & 7) | ((((i >> 3) + d) & 3) << 3)


def hi_flip(i):
    return i ^ 1


def x_shift(d):
    return lambda i: (i & 1) | ((((i >> 1) + d) & 3) << 1)


def z_flip(bit):
    return lambda i: i ^ (2 << bit)


def join(mine, other, bit):
    return jnp.where(bit == 0, jnp.stack([mine, other]), jnp.stack([other, mine]))


def around_z(value, here):
    for bit in range(2):
        value = join(value, permute(value, "chan", z_flip(bit)), (here >> bit) & 1)
    return value.reshape((4,) + value.shape[2:])


def around_y(value, here):
    after, before = permute(value, "chan", y_shift(1)), permute(value, "chan", y_shift(3))
    value, after, before = lax.optimization_barrier((value, after, before))
    ring = [value, after, permute(value, "chan", y_shift(2)), before]
    ring = jnp.stack(ring[::-1] + ring[::-1])
    return lax.dynamic_slice_in_dim(ring, 3 - here, 4, 0)


def correlate_kernel(place_ref, owners_ref, mask_ref, *refs, span, chunk):
    own_refs, block_refs = refs[:2], refs[2:10]
    out_ref, own, block, left, right, total = refs[10:]
    chan, win = place_ref[0], place_ref[1]
    core, x, hi = chan & 1, win >> 1, win & 1
    rows = own.shape[0]
    share = rows // STEPS
    width = block.shape[0]
    length = block.shape[1] - EDGE
    quarter = span // 4
    bf16 = jnp.bfloat16

    own[:, :EDGE] = jnp.zeros((rows, EDGE), bf16)
    own[:, EDGE + length:] = jnp.zeros((rows, EDGE), bf16)
    block[:, length:] = jnp.zeros((width, EDGE), bf16)
    own_power = jnp.zeros((rows, EDGE), jnp.float32)
    slices = length // span
    for k in range(4 * slices):
        d, half, w = k // (2 * slices), k // slices % 2, k % slices
        where = 2 * half + (core ^ d)
        at = (half * slices + w) * quarter
        piece = own_refs[d][:, at:at + quarter]
        start = pl.multiple_of(EDGE + w * span + where * quarter, EDGE)
        own[:, pl.ds(start, quarter)] = piece
        wide = piece.astype(jnp.float32)
        for k in range(quarter // EDGE):
            part = wide[:, k * EDGE:(k + 1) * EDGE]
            own_power += part * part
    block_power = jnp.zeros((width, EDGE), jnp.float32)
    for d in range(8):
        piece = block_refs[d][...]
        slot = (((x - d) & 3) << 1) | (hi if d < 4 else 1 - hi)
        start = pl.multiple_of(slot * span, EDGE)
        block[:, pl.ds(start, span)] = piece
        wide = piece.astype(jnp.float32)
        for k in range(span // EDGE):
            part = wide[:, k * EDGE:(k + 1) * EDGE]
            block_power += part * part
    own_power = jnp.sum(own_power, axis=1, keepdims=True) / length
    block_power = jnp.sum(block_power, axis=1, keepdims=True) / length
    own_scale = 1.0 / jnp.sqrt(own_power + 1e-06)
    block_scale = 1.0 / jnp.sqrt(block_power + 1e-06)
    block_scale = jnp.transpose(jnp.broadcast_to(block_scale, (width, width)))[:1]

    def product(a, b):
        return lax.dot_general(a, b, (((1,), (1,)), ((), ())), preferred_element_type=jnp.float32)

    lead = own[:, :2 * EDGE]
    before = jnp.concatenate([jnp.zeros((width, EDGE - HALF), bf16), block[:, :HALF]], axis=1)
    part = HALF * share
    flags = [mask_ref[owners_ref[s], chan] for s in range(STEPS)]
    for k in range(0, length, chunk):
        right[:width] = block[:, k:k + chunk]
        right[width:] = block[:, HALF + k:HALF + k + chunk]
        for s in range(STEPS):
            @pl.when(flags[s] != 0)
            def _():
                if k == 0:
                    for l in range(HALF):
                        left[l * share:(l + 1) * share, :EDGE] = lead[s * share:(s + 1) * share, LAG - l:LAG - l + EDGE]
                    at = slice(s * part, (s + 1) * part)
                    total[at, :width] = jnp.zeros((part, width), jnp.float32)
                    total[at, width:] = product(left[:, :EDGE], before)
                mine = own[s * share:(s + 1) * share, k + EDGE:k + chunk + 2 * EDGE]
                for g in range(0, HALF, 21):
                    stop = min(g + 21, HALF)
                    for l in range(g, stop):
                        left[l * share:(l + 1) * share] = mine[:, LAG - l:LAG - l + chunk]
                    at = slice(s * part + g * share, s * part + stop * share)
                    total[at] += product(left[g * share:stop * share], right[...])

    norm = 1.0 / math.sqrt(length)
    for s in range(STEPS):
        scale = own_scale[s * share:(s + 1) * share] * (block_scale * norm)

        @pl.when(flags[s] != 0)
        def _():
            wide = scale * flags[s].astype(jnp.float32)
            for l in range(HALF):
                at = slice(s * part + l * share, s * part + (l + 1) * share)
                out_ref[s, l] = total[at, :width] * wide
                if l + HALF < LAGS:
                    out_ref[s, l + HALF] = total[at, width:] * wide

        @pl.when(flags[s] == 0)
        def _():
            out_ref[s] = jnp.zeros((LAGS, share, width), jnp.float32)


def correlate(place, owners, pair_mask, own, block):
    rows, width, span = own[0].shape[0], block[0].shape[0], block[0].shape[1]
    length = span * len(block)
    chunk = 12288
    vmem = pl.BlockSpec(memory_space=pltpu.VMEM)
    return pl.pallas_call(
        functools.partial(correlate_kernel, span=span, chunk=chunk),
        out_shape=jax.ShapeDtypeStruct((STEPS, LAGS, rows // STEPS, width), jnp.float32),
        in_specs=[pl.BlockSpec(memory_space=pltpu.SMEM)] * 3 + [vmem] * 10,
        out_specs=vmem,
        scratch_shapes=[
            pltpu.VMEM((rows, length + 2 * EDGE), jnp.bfloat16),
            pltpu.VMEM((width, length + EDGE), jnp.bfloat16),
            pltpu.VMEM((HALF * rows // STEPS, chunk), jnp.bfloat16),
            pltpu.VMEM((2 * width, chunk), jnp.bfloat16),
            pltpu.VMEM((HALF * rows, 2 * width), jnp.float32),
        ],
        compiler_params=pltpu.CompilerParams(vmem_limit_bytes=56 * 2**20),
        cost_estimate=pl.CostEstimate(
            flops=2 * HALF * rows * 2 * width * length, bytes_accessed=6 * 2**20, transcendentals=0
        ),
    )(place, owners, pair_mask, *own, *block)


def local(record, owners, pair_mask):
    width, span = record.shape
    channels = width * lax.axis_size("chan")
    chan, win = lax.axis_index("chan"), lax.axis_index("win")

    sums = jnp.sum(record, axis=0)
    sums = sums + permute(sums, "chan", core_flip)
    sums = sums + (permute(sums, "chan", z_shift(1)) + permute(sums, "chan", z_shift(2)) + permute(sums, "chan", z_shift(3)))
    sums = sums + (permute(sums, "chan", y_shift(1)) + permute(sums, "chan", y_shift(2)) + permute(sums, "chan", y_shift(3)))
    cleaned = (record - (sums / channels)[None, :]).astype(jnp.bfloat16)

    far = permute(cleaned, "win", hi_flip)
    block = [cleaned] + [permute(cleaned, "win", x_shift(d)) for d in (1, 2, 3)]

    quarter = span // 4
    here = chan >= 0

    def take(value):
        pieces = value.reshape(8, 4, 2, 2, 2, 2, quarter).transpose(4, 2, 1, 5, 0, 3, 6).reshape(256, 2, quarter)
        pieces = lax.all_to_all(pieces, ("chan", "win"), 0, 0).reshape(32, 8, 2, quarter)
        chosen = owners[:, None] == jnp.arange(32, dtype=owners.dtype)
        pieces = jnp.where(chosen[:, :, None, None, None], pieces, jnp.zeros_like(pieces)).astype(jnp.float32)
        return jnp.sum(pieces, axis=1).astype(jnp.bfloat16)

    mine = lax.cond(here, take, lambda value: jnp.zeros((STEPS, 8, 2, quarter), jnp.bfloat16), cleaned)
    place = jnp.stack([chan, win])
    mine, place, far, *block = lax.optimization_barrier((mine, place, far, *block))
    block += [far] + [permute(far, "win", x_shift(d)) for d in (1, 2, 3)]

    def share(value):
        value = around_z(value, (chan >> 1) & 3)
        value = around_y(value, chan >> 3).reshape(2, 2, 4, STEPS, 8, 2, quarter)
        value = value.transpose(3, 2, 1, 5, 0, 4, 6).reshape(16 * STEPS, 2 * 8 * quarter)
        return value, permute(value, "chan", core_flip)

    def none(value):
        blank = jnp.zeros((16 * STEPS, 2 * 8 * quarter), jnp.bfloat16)
        return blank, blank

    own = lax.cond(here, share, none, mine)
    own, *block = lax.optimization_barrier((own, *block))
    return correlate(place, owners, pair_mask, own, block)


def solution(mesh):
    in_specs = (P("chan", "win"), P(), P())
    out_specs = P(None, None, "win", "chan")
    return jax.shard_map(local, mesh=mesh, in_specs=in_specs, out_specs=out_specs, check_vma=False)
```

```python
import functools
import math

import jax
import jax.numpy as jnp
from jax import lax
from jax.experimental import pallas as pl
from jax.experimental.pallas import tpu as pltpu
from jax.sharding import PartitionSpec as P

LAG = 40
STEPS = 3
LAGS = 2 * LAG + 1
HALF = LAG + 1
EDGE = 128
GROUP = 21


def permute(value, axis, target):
    size = lax.axis_size(axis)
    return lax.ppermute(value, axis, [(i, target(i)) for i in range(size)])


def core_flip(i):
    return i ^ 1


def z_shift(d):
    return lambda i: (i & ~6) | ((((i >> 1) + d) & 3) << 1)


def y_shift(d):
    return lambda i: (i & 7) | ((((i >> 3) + d) & 3) << 3)


def hi_flip(i):
    return i ^ 1


def x_shift(d):
    return lambda i: (i & 1) | ((((i >> 1) + d) & 3) << 1)


def around(value, shift, here):
    ring = [value] + [permute(value, "chan", shift(d)) for d in (1, 2, 3)]
    ring = jnp.stack(ring[::-1] + ring[::-1])
    return lax.dynamic_slice_in_dim(ring, 3 - here, 4, 0)


def correlate_kernel(place_ref, owners_ref, mask_ref, *refs, span):
    own_refs, block_refs = refs[:2], refs[2:11]
    out_ref, own, left, right, total, result, read, write = refs[11:]
    chan, win = place_ref[0], place_ref[1]
    core, x, hi = chan & 1, win >> 1, win & 1
    rows = own.shape[0]
    share = rows // STEPS
    length = right.shape[1]
    width = right.shape[0] // 2
    slices = length // span
    quarter = span // 4
    bf16 = jnp.bfloat16

    copies = []

    def bring(source, target):
        copy = pltpu.make_async_copy(source, target, read.at[len(copies)])
        copy.start()
        copies.append(copy)

    for k in range(4 * slices):
        d, half, w = k // (2 * slices), k // slices % 2, k % slices
        where = 2 * half + (core ^ d)
        at = (half * slices + w) * quarter
        start = pl.multiple_of(EDGE + w * span + where * quarter, EDGE)
        bring(own_refs[d].at[:, at:at + quarter], own.at[:, pl.ds(start, quarter)])
    order = ((0, 0), (1, 0), (2, 0), (3, 0), (0, 1), (1, 1), (3, 1), (2, 1), (2, 1))
    starts = []
    for d, (step, flip) in enumerate(order):
        slot = (((x - step) & 3) << 1) | (1 - hi if flip else hi)
        starts.append(pl.multiple_of(slot * span, EDGE))
        top = width // 2 if d == 8 else 0
        tall = block_refs[d].shape[0]
        bring(block_refs[d], right.at[top:top + tall, pl.ds(starts[d], span)])
    own[:, :EDGE] = jnp.zeros((rows, EDGE), bf16)
    own[:, EDGE + length:] = jnp.zeros((rows, EDGE), bf16)

    def power(piece):
        total = jnp.zeros((piece.shape[0], EDGE), jnp.float32)
        for k in range(piece.shape[1] // EDGE):
            part = piece[:, k * EDGE:(k + 1) * EDGE].astype(jnp.float32)
            total += part * part
        return total

    for copy in copies[:4 * slices]:
        copy.wait()
    own_power = power(own[:, EDGE:EDGE + length])
    for copy in copies[4 * slices:]:
        copy.wait()
    block_power = power(right[:width])
    own_power = jnp.sum(own_power, axis=1, keepdims=True) / length
    block_power = jnp.sum(block_power, axis=1, keepdims=True) / length
    own_scale = 1.0 / jnp.sqrt(own_power + 1e-06)
    block_scale = 1.0 / jnp.sqrt(block_power + 1e-06)
    block_scale = jnp.transpose(jnp.broadcast_to(block_scale, (width, width)))[:1]
    right[width:, :length - EDGE] = right[:width, HALF:length - EDGE + HALF]
    right[width:, length - EDGE:] = jnp.concatenate(
        [right[:width, length - EDGE + HALF:], jnp.zeros((width, HALF), bf16)], axis=1
    )

    def product(a, b):
        return lax.dot_general(a, b, (((1,), (1,)), ((), ())), preferred_element_type=jnp.float32)

    before = jnp.concatenate([jnp.zeros((width, EDGE - HALF), bf16), right[:width, :HALF]], axis=1)
    part = HALF * share
    norm = 1.0 / math.sqrt(length)
    writes = []
    for s in range(STEPS):
        mine = slice(s * share, (s + 1) * share)
        flag = mask_ref[owners_ref[s], chan]

        @pl.when(flag != 0)
        def _():
            lead = own[mine, :2 * EDGE]
            for l in range(HALF):
                left[l * share:(l + 1) * share, :EDGE] = lead[:, LAG - l:LAG - l + EDGE]
            total[:, :width] = jnp.zeros((part, width), jnp.float32)
            total[:, width:] = product(left[:, :EDGE], before)
            source = own[mine, EDGE:]
            for g in range(0, HALF, GROUP):
                stop = min(g + GROUP, HALF)
                for l in range(g, stop):
                    left[l * share:(l + 1) * share] = source[:, LAG - l:LAG - l + length]
                at = slice(g * share, stop * share)
                total[at] += product(left[at], right[...])
            scale = own_scale[mine] * (block_scale * (norm * flag.astype(jnp.float32)))
            for l in range(HALF):
                at = slice(l * share, (l + 1) * share)
                result[s, l] = total[at, :width] * scale
                if l + HALF < LAGS:
                    result[s, l + HALF] = total[at, width:] * scale

        @pl.when(flag == 0)
        def _():
            result[s] = jnp.zeros((LAGS, share, width), jnp.float32)

        writes.append(pltpu.make_async_copy(result.at[s], out_ref.at[s], write.at[s]))
        writes[s].start()
    for copy in writes:
        copy.wait()


def correlate(place, owners, pair_mask, own, block):
    rows, width, span = own[0].shape[0], block[0].shape[0], block[0].shape[1]
    length = 2 * own[0].shape[1]
    share = rows // STEPS
    there = pl.BlockSpec(memory_space=pl.ANY)
    return pl.pallas_call(
        functools.partial(correlate_kernel, span=span),
        out_shape=jax.ShapeDtypeStruct((STEPS, LAGS, share, width), jnp.float32),
        in_specs=[pl.BlockSpec(memory_space=pltpu.SMEM)] * 3 + [there] * 11,
        out_specs=there,
        scratch_shapes=[
            pltpu.VMEM((rows, length + 2 * EDGE), jnp.bfloat16),
            pltpu.VMEM((HALF * share, length), jnp.bfloat16),
            pltpu.VMEM((2 * width, length), jnp.bfloat16),
            pltpu.VMEM((HALF * share, 2 * width), jnp.float32),
            pltpu.VMEM((STEPS, LAGS, share, width), jnp.float32),
            pltpu.SemaphoreType.DMA((4 * (length // span) + 9,)),
            pltpu.SemaphoreType.DMA((STEPS,)),
        ],
        compiler_params=pltpu.CompilerParams(vmem_limit_bytes=44 * 2**20),
        cost_estimate=pl.CostEstimate(
            flops=2 * HALF * rows * 2 * width * length, bytes_accessed=6 * 2**20, transcendentals=0
        ),
    )(place, owners, pair_mask, *own, *block)


def local(record, owners, pair_mask):
    width, span = record.shape
    channels = width * lax.axis_size("chan")
    chan, win = lax.axis_index("chan"), lax.axis_index("win")

    sums = jnp.sum(record, axis=0)
    sums = sums + permute(sums, "chan", core_flip)
    sums = sums + (permute(sums, "chan", z_shift(1)) + permute(sums, "chan", z_shift(2)) + permute(sums, "chan", z_shift(3)))
    sums = sums + (permute(sums, "chan", y_shift(1)) + permute(sums, "chan", y_shift(2)) + permute(sums, "chan", y_shift(3)))
    cleaned = (record - (sums / channels)[None, :]).astype(jnp.bfloat16)

    far = permute(cleaned, "win", hi_flip)
    block = [cleaned] + [permute(cleaned, "win", x_shift(d)) for d in (1, 2, 3)]

    quarter = span // 4
    here = chan >= 0

    def take(value):
        pieces = value.reshape(8, 4, 2, 2, 2, 2, quarter).transpose(4, 2, 1, 5, 0, 3, 6).reshape(256, 2, quarter)
        pieces = lax.all_to_all(pieces, ("chan", "win"), 0, 0).reshape(32, 8, 2, quarter)
        chosen = owners[:, None] == jnp.arange(32, dtype=owners.dtype)
        pieces = jnp.where(chosen[:, :, None, None, None], pieces, jnp.zeros_like(pieces)).astype(jnp.float32)
        return jnp.sum(pieces, axis=1).astype(jnp.bfloat16)

    mine = lax.cond(here, take, lambda value: jnp.zeros((STEPS, 8, 2, quarter), jnp.bfloat16), cleaned)
    place = jnp.stack([chan, win])
    mine, place, far, *block = lax.optimization_barrier((mine, place, far, *block))
    after, before = permute(far, "win", x_shift(1)), permute(far, "win", x_shift(3))
    blank = jnp.zeros((4, STEPS, 8, 2, quarter), jnp.bfloat16)
    mine = lax.cond(here, lambda value: around(value, z_shift, (chan >> 1) & 3), lambda value: blank, mine)
    mine, after, before = lax.optimization_barrier((mine, after, before))
    half = width // 2
    across = [permute(after[:half], "win", x_shift(1)), permute(before[half:], "win", x_shift(3))]

    def share(value):
        value = around(value, y_shift, chan >> 3).reshape(2, 2, 4, STEPS, 8, 2, quarter)
        value = value.transpose(3, 2, 1, 5, 0, 4, 6).reshape(16 * STEPS, 2 * 8 * quarter)
        return value, permute(value, "chan", core_flip)

    def none(value):
        blank = jnp.zeros((16 * STEPS, 2 * 8 * quarter), jnp.bfloat16)
        return blank, blank

    own = lax.cond(here, share, none, mine)
    own, across = lax.optimization_barrier((own, across))
    block += [far, after, before] + across
    return correlate(place, owners, pair_mask, own, block)


def solution(mesh):
    in_specs = (P("chan", "win"), P(), P())
    out_specs = P(None, None, "win", "chan")
    return jax.shard_map(local, mesh=mesh, in_specs=in_specs, out_specs=out_specs, check_vma=False)
```

```python
import functools
import math

import jax
import jax.numpy as jnp
from jax import lax
from jax.experimental import pallas as pl
from jax.experimental.pallas import tpu as pltpu
from jax.sharding import PartitionSpec as P

LAG = 40
STEPS = 3
LAGS = 2 * LAG + 1
HALF = LAG + 1
EDGE = 128
GROUP = 21


def permute(value, axis, target):
    size = lax.axis_size(axis)
    return lax.ppermute(value, axis, [(i, target(i)) for i in range(size)])


def core_flip(i):
    return i ^ 1


def z_shift(d):
    return lambda i: (i & ~6) | ((((i >> 1) + d) & 3) << 1)


def y_shift(d):
    return lambda i: (i & 7) | ((((i >> 3) + d) & 3) << 3)


def hi_flip(i):
    return i ^ 1


def x_shift(d):
    return lambda i: (i & 1) | ((((i >> 1) + d) & 3) << 1)


def around(value, shift, here):
    ring = [value] + [permute(value, "chan", shift(d)) for d in (1, 2, 3)]
    ring = jnp.stack(ring[::-1] + ring[::-1])
    return lax.dynamic_slice_in_dim(ring, 3 - here, 4, 0)


def correlate_kernel(place_ref, owners_ref, mask_ref, *refs, span):
    own_refs, block_refs = refs[:2], refs[2:11]
    out_ref, own, left, right, total, result, write = refs[11:]
    chan, win = place_ref[0], place_ref[1]
    core, x, hi = chan & 1, win >> 1, win & 1
    rows = own.shape[0]
    share = rows // STEPS
    length = right.shape[1]
    width = right.shape[0] // 2
    slices = length // span
    quarter = span // 4
    bf16 = jnp.bfloat16


    def bring(source, target):
        target[...] = source[...]

    for k in range(4 * slices):
        d, half, w = k // (2 * slices), k // slices % 2, k % slices
        where = 2 * half + (core ^ d)
        at = (half * slices + w) * quarter
        start = pl.multiple_of(EDGE + w * span + where * quarter, EDGE)
        bring(own_refs[d].at[:, at:at + quarter], own.at[:, pl.ds(start, quarter)])
    order = ((0, 0), (1, 0), (2, 0), (3, 0), (0, 1), (1, 1), (3, 1), (2, 1), (2, 1))
    starts = []
    for d, (step, flip) in enumerate(order):
        slot = (((x - step) & 3) << 1) | (1 - hi if flip else hi)
        starts.append(pl.multiple_of(slot * span, EDGE))
        top = width // 2 if d == 8 else 0
        tall = block_refs[d].shape[0]
        bring(block_refs[d], right.at[top:top + tall, pl.ds(starts[d], span)])
    own[:, :EDGE] = jnp.zeros((rows, EDGE), bf16)
    own[:, EDGE + length:] = jnp.zeros((rows, EDGE), bf16)

    def power(piece):
        total = jnp.zeros((piece.shape[0], EDGE), jnp.float32)
        for k in range(piece.shape[1] // EDGE):
            part = piece[:, k * EDGE:(k + 1) * EDGE].astype(jnp.float32)
            total += part * part
        return total

    own_power = power(own[:, EDGE:EDGE + length])
    block_power = power(right[:width])
    own_power = jnp.sum(own_power, axis=1, keepdims=True) / length
    block_power = jnp.sum(block_power, axis=1, keepdims=True) / length
    own_scale = 1.0 / jnp.sqrt(own_power + 1e-06)
    block_scale = 1.0 / jnp.sqrt(block_power + 1e-06)
    block_scale = jnp.transpose(jnp.broadcast_to(block_scale, (width, width)))[:1]
    right[width:, :length - EDGE] = right[:width, HALF:length - EDGE + HALF]
    right[width:, length - EDGE:] = jnp.concatenate(
        [right[:width, length - EDGE + HALF:], jnp.zeros((width, HALF), bf16)], axis=1
    )

    def product(a, b):
        return lax.dot_general(a, b, (((1,), (1,)), ((), ())), preferred_element_type=jnp.float32)

    before = jnp.concatenate([jnp.zeros((width, EDGE - HALF), bf16), right[:width, :HALF]], axis=1)
    part = HALF * share
    norm = 1.0 / math.sqrt(length)
    writes = []
    for s in range(STEPS):
        mine = slice(s * share, (s + 1) * share)
        flag = mask_ref[owners_ref[s], chan]

        @pl.when(flag != 0)
        def _():
            lead = own[mine, :2 * EDGE]
            for l in range(HALF):
                left[l * share:(l + 1) * share, :EDGE] = lead[:, LAG - l:LAG - l + EDGE]
            total[:, :width] = jnp.zeros((part, width), jnp.float32)
            total[:, width:] = product(left[:, :EDGE], before)
            source = own[mine, EDGE:]
            for g in range(0, HALF, GROUP):
                stop = min(g + GROUP, HALF)
                for l in range(g, stop):
                    left[l * share:(l + 1) * share] = source[:, LAG - l:LAG - l + length]
                at = slice(g * share, stop * share)
                total[at] += product(left[at], right[...])
            scale = own_scale[mine] * (block_scale * (norm * flag.astype(jnp.float32)))
            for l in range(HALF):
                at = slice(l * share, (l + 1) * share)
                result[s, l] = total[at, :width] * scale
                if l + HALF < LAGS:
                    result[s, l + HALF] = total[at, width:] * scale

        @pl.when(flag == 0)
        def _():
            result[s] = jnp.zeros((LAGS, share, width), jnp.float32)

        writes.append(pltpu.make_async_copy(result.at[s], out_ref.at[s], write.at[s]))
        writes[s].start()
    for copy in writes:
        copy.wait()


def correlate(place, owners, pair_mask, own, block):
    rows, width, span = own[0].shape[0], block[0].shape[0], block[0].shape[1]
    length = 2 * own[0].shape[1]
    share = rows // STEPS
    there = pl.BlockSpec(memory_space=pl.ANY)
    return pl.pallas_call(
        functools.partial(correlate_kernel, span=span),
        out_shape=jax.ShapeDtypeStruct((STEPS, LAGS, share, width), jnp.float32),
        in_specs=[pl.BlockSpec(memory_space=pltpu.SMEM)] * 3 + [pl.BlockSpec(memory_space=pltpu.VMEM)] * 11,
        out_specs=there,
        scratch_shapes=[
            pltpu.VMEM((rows, length + 2 * EDGE), jnp.bfloat16),
            pltpu.VMEM((HALF * share, length), jnp.bfloat16),
            pltpu.VMEM((2 * width, length), jnp.bfloat16),
            pltpu.VMEM((HALF * share, 2 * width), jnp.float32),
            pltpu.VMEM((STEPS, LAGS, share, width), jnp.float32),
            pltpu.SemaphoreType.DMA((STEPS,)),
        ],
        compiler_params=pltpu.CompilerParams(vmem_limit_bytes=56 * 2**20),
        cost_estimate=pl.CostEstimate(
            flops=2 * HALF * rows * 2 * width * length, bytes_accessed=6 * 2**20, transcendentals=0
        ),
    )(place, owners, pair_mask, *own, *block)


def local(record, owners, pair_mask):
    width, span = record.shape
    channels = width * lax.axis_size("chan")
    chan, win = lax.axis_index("chan"), lax.axis_index("win")

    sums = jnp.sum(record, axis=0)
    sums = sums + permute(sums, "chan", core_flip)
    sums = sums + (permute(sums, "chan", z_shift(1)) + permute(sums, "chan", z_shift(2)) + permute(sums, "chan", z_shift(3)))
    sums = sums + (permute(sums, "chan", y_shift(1)) + permute(sums, "chan", y_shift(2)) + permute(sums, "chan", y_shift(3)))
    cleaned = (record - (sums / channels)[None, :]).astype(jnp.bfloat16)

    far = permute(cleaned, "win", hi_flip)
    block = [cleaned] + [permute(cleaned, "win", x_shift(d)) for d in (1, 2, 3)]

    quarter = span // 4
    here = chan >= 0

    def take(value):
        pieces = value.reshape(8, 4, 2, 2, 2, 2, quarter).transpose(4, 2, 1, 5, 0, 3, 6).reshape(256, 2, quarter)
        pieces = lax.all_to_all(pieces, ("chan", "win"), 0, 0).reshape(32, 8, 2, quarter)
        chosen = owners[:, None] == jnp.arange(32, dtype=owners.dtype)
        pieces = jnp.where(chosen[:, :, None, None, None], pieces, jnp.zeros_like(pieces)).astype(jnp.float32)
        return jnp.sum(pieces, axis=1).astype(jnp.bfloat16)

    mine = lax.cond(here, take, lambda value: jnp.zeros((STEPS, 8, 2, quarter), jnp.bfloat16), cleaned)
    place = jnp.stack([chan, win])
    mine, place, far, *block = lax.optimization_barrier((mine, place, far, *block))
    after, before = permute(far, "win", x_shift(1)), permute(far, "win", x_shift(3))
    blank = jnp.zeros((4, STEPS, 8, 2, quarter), jnp.bfloat16)
    mine = lax.cond(here, lambda value: around(value, z_shift, (chan >> 1) & 3), lambda value: blank, mine)
    mine, after, before = lax.optimization_barrier((mine, after, before))
    half = width // 2
    across = [permute(after[:half], "win", x_shift(1)), permute(before[half:], "win", x_shift(3))]

    def share(value):
        value = around(value, y_shift, chan >> 3).reshape(2, 2, 4, STEPS, 8, 2, quarter)
        value = value.transpose(3, 2, 1, 5, 0, 4, 6).reshape(16 * STEPS, 2 * 8 * quarter)
        return value, permute(value, "chan", core_flip)

    def none(value):
        blank = jnp.zeros((16 * STEPS, 2 * 8 * quarter), jnp.bfloat16)
        return blank, blank

    own = lax.cond(here, share, none, mine)
    own, across = lax.optimization_barrier((own, across))
    block += [far, after, before] + across
    return correlate(place, owners, pair_mask, own, block)


def solution(mesh):
    in_specs = (P("chan", "win"), P(), P())
    out_specs = P(None, None, "win", "chan")
    return jax.shard_map(local, mesh=mesh, in_specs=in_specs, out_specs=out_specs, check_vma=False)
```

```python
import functools
import math

import jax
import jax.numpy as jnp
from jax import lax
from jax.experimental import pallas as pl
from jax.experimental.pallas import tpu as pltpu
from jax.sharding import PartitionSpec as P

LAG = 40
STEPS = 3
LAGS = 2 * LAG + 1
HALF = LAG + 1
EDGE = 128
GROUP = 21


def permute(value, axis, target):
    size = lax.axis_size(axis)
    return lax.ppermute(value, axis, [(i, target(i)) for i in range(size)])


def core_flip(i):
    return i ^ 1


def z_shift(d):
    return lambda i: (i & ~6) | ((((i >> 1) + d) & 3) << 1)


def y_shift(d):
    return lambda i: (i & 7) | ((((i >> 3) + d) & 3) << 3)


def hi_flip(i):
    return i ^ 1


def x_shift(d):
    return lambda i: (i & 1) | ((((i >> 1) + d) & 3) << 1)


def around(value, shift, here):
    ring = [value] + [permute(value, "chan", shift(d)) for d in (1, 2, 3)]
    ring = jnp.stack(ring[::-1] + ring[::-1])
    return lax.dynamic_slice_in_dim(ring, 3 - here, 4, 0)


def correlate_kernel(owners_ref, mask_ref, *refs, span):
    own_refs, block_refs = refs[:2], refs[2:11]
    out_ref, own, left, right, total, result, write = refs[11:]
    chan, win = lax.axis_index("chan"), lax.axis_index("win")
    core, x, hi = chan & 1, win >> 1, win & 1
    rows = own.shape[0]
    share = rows // STEPS
    length = right.shape[1]
    width = right.shape[0] // 2
    slices = length // span
    quarter = span // 4
    bf16 = jnp.bfloat16


    def bring(source, target):
        target[...] = source[...]

    for k in range(4 * slices):
        d, half, w = k // (2 * slices), k // slices % 2, k % slices
        where = 2 * half + (core ^ d)
        at = (half * slices + w) * quarter
        start = pl.multiple_of(EDGE + w * span + where * quarter, EDGE)
        bring(own_refs[d].at[:, at:at + quarter], own.at[:, pl.ds(start, quarter)])
    order = ((0, 0), (1, 0), (2, 0), (3, 0), (0, 1), (1, 1), (3, 1), (2, 1), (2, 1))
    starts = []
    for d, (step, flip) in enumerate(order):
        slot = (((x - step) & 3) << 1) | (1 - hi if flip else hi)
        starts.append(pl.multiple_of(slot * span, EDGE))
        top = width // 2 if d == 8 else 0
        tall = block_refs[d].shape[0]
        bring(block_refs[d], right.at[top:top + tall, pl.ds(starts[d], span)])
    own[:, :EDGE] = jnp.zeros((rows, EDGE), bf16)
    own[:, EDGE + length:] = jnp.zeros((rows, EDGE), bf16)

    def power(piece):
        total = jnp.zeros((piece.shape[0], EDGE), jnp.float32)
        for k in range(piece.shape[1] // EDGE):
            part = piece[:, k * EDGE:(k + 1) * EDGE].astype(jnp.float32)
            total += part * part
        return total

    own_power = power(own[:, EDGE:EDGE + length])
    block_power = power(right[:width])
    own_power = jnp.sum(own_power, axis=1, keepdims=True) / length
    block_power = jnp.sum(block_power, axis=1, keepdims=True) / length
    own_scale = 1.0 / jnp.sqrt(own_power + 1e-06)
    block_scale = 1.0 / jnp.sqrt(block_power + 1e-06)
    block_scale = jnp.transpose(jnp.broadcast_to(block_scale, (width, width)))[:1]
    right[width:, :length - EDGE] = right[:width, HALF:length - EDGE + HALF]
    right[width:, length - EDGE:] = jnp.concatenate(
        [right[:width, length - EDGE + HALF:], jnp.zeros((width, HALF), bf16)], axis=1
    )

    def product(a, b):
        return lax.dot_general(a, b, (((1,), (1,)), ((), ())), preferred_element_type=jnp.float32)

    before = jnp.concatenate([jnp.zeros((width, EDGE - HALF), bf16), right[:width, :HALF]], axis=1)
    norm = 1.0 / math.sqrt(length)
    writes = []
    for s in range(STEPS):
        mine = slice(s * share, (s + 1) * share)
        flag = mask_ref[owners_ref[s], chan]

        @pl.when(flag != 0)
        def _():
            lead = own[mine, :2 * EDGE]
            for l in range(HALF):
                left[l * share:(l + 1) * share, :EDGE] = lead[:, LAG - l:LAG - l + EDGE]
            total[:, width:] = product(left[:, :EDGE], before)
            source = own[mine, EDGE:]
            for g in range(0, HALF, GROUP):
                stop = min(g + GROUP, HALF)
                for l in range(g, stop):
                    left[l * share:(l + 1) * share] = source[:, LAG - l:LAG - l + length]
                at = slice(g * share, stop * share)
                sums = product(left[at], right[...])
                total[at, :width] = sums[:, :width]
                total[at, width:] += sums[:, width:]
            scale = own_scale[mine] * (block_scale * (norm * flag.astype(jnp.float32)))
            for l in range(HALF):
                at = slice(l * share, (l + 1) * share)
                result[s, l] = total[at, :width] * scale
                if l + HALF < LAGS:
                    result[s, l + HALF] = total[at, width:] * scale

        @pl.when(flag == 0)
        def _():
            result[s] = jnp.zeros((LAGS, share, width), jnp.float32)

        writes.append(pltpu.make_async_copy(result.at[s], out_ref.at[s], write.at[s]))
        writes[s].start()
    for copy in writes:
        copy.wait()


def correlate(owners, pair_mask, own, block):
    rows, width, span = own[0].shape[0], block[0].shape[0], block[0].shape[1]
    length = 2 * own[0].shape[1]
    share = rows // STEPS
    there = pl.BlockSpec(memory_space=pl.ANY)
    return pl.pallas_call(
        functools.partial(correlate_kernel, span=span),
        out_shape=jax.ShapeDtypeStruct((STEPS, LAGS, share, width), jnp.float32),
        in_specs=[pl.BlockSpec(memory_space=pltpu.SMEM)] * 2 + [pl.BlockSpec(memory_space=pltpu.VMEM)] * 11,
        out_specs=there,
        scratch_shapes=[
            pltpu.VMEM((rows, length + 2 * EDGE), jnp.bfloat16),
            pltpu.VMEM((HALF * share, length), jnp.bfloat16),
            pltpu.VMEM((2 * width, length), jnp.bfloat16),
            pltpu.VMEM((HALF * share, 2 * width), jnp.float32),
            pltpu.VMEM((STEPS, LAGS, share, width), jnp.float32),
            pltpu.SemaphoreType.DMA((STEPS,)),
        ],
        compiler_params=pltpu.CompilerParams(vmem_limit_bytes=56 * 2**20),
        cost_estimate=pl.CostEstimate(
            flops=2 * HALF * rows * 2 * width * length, bytes_accessed=6 * 2**20, transcendentals=0
        ),
    )(owners, pair_mask, *own, *block)


def local(record, owners, pair_mask):
    width, span = record.shape
    channels = width * lax.axis_size("chan")
    chan, win = lax.axis_index("chan"), lax.axis_index("win")

    sums = jnp.sum(record, axis=0)
    sums = sums + permute(sums, "chan", core_flip)
    sums = sums + (permute(sums, "chan", z_shift(1)) + permute(sums, "chan", z_shift(2)) + permute(sums, "chan", z_shift(3)))
    sums = sums + (permute(sums, "chan", y_shift(1)) + permute(sums, "chan", y_shift(2)) + permute(sums, "chan", y_shift(3)))
    cleaned = (record - (sums / channels)[None, :]).astype(jnp.bfloat16)

    far = permute(cleaned, "win", hi_flip)
    block = [cleaned] + [permute(cleaned, "win", x_shift(d)) for d in (1, 2, 3)]

    quarter = span // 4
    here = chan >= 0

    def take(value):
        pieces = value.reshape(8, 4, 2, 2, 2, 2, quarter).transpose(4, 2, 1, 5, 0, 3, 6).reshape(256, 2, quarter)
        pieces = lax.all_to_all(pieces, ("chan", "win"), 0, 0).reshape(32, 8, 2, quarter)
        chosen = owners[:, None] == jnp.arange(32, dtype=owners.dtype)
        pieces = jnp.where(chosen[:, :, None, None, None], pieces, jnp.zeros_like(pieces)).astype(jnp.float32)
        return jnp.sum(pieces, axis=1).astype(jnp.bfloat16)

    mine = lax.cond(here, take, lambda value: jnp.zeros((STEPS, 8, 2, quarter), jnp.bfloat16), cleaned)
    mine, far, *block = lax.optimization_barrier((mine, far, *block))
    after, before = permute(far, "win", x_shift(1)), permute(far, "win", x_shift(3))
    blank = jnp.zeros((4, STEPS, 8, 2, quarter), jnp.bfloat16)
    mine = lax.cond(here, lambda value: around(value, z_shift, (chan >> 1) & 3), lambda value: blank, mine)
    mine, after, before = lax.optimization_barrier((mine, after, before))
    half = width // 2
    across = [permute(after[:half], "win", x_shift(1)), permute(before[half:], "win", x_shift(3))]

    def share(value):
        value = around(value, y_shift, chan >> 3).reshape(2, 2, 4, STEPS, 8, 2, quarter)
        value = value.transpose(3, 2, 1, 5, 0, 4, 6).reshape(16 * STEPS, 2 * 8 * quarter)
        return value, permute(value, "chan", core_flip)

    def none(value):
        blank = jnp.zeros((16 * STEPS, 2 * 8 * quarter), jnp.bfloat16)
        return blank, blank

    own = lax.cond(here, share, none, mine)
    own, across = lax.optimization_barrier((own, across))
    block += [far, after, before] + across
    return correlate(owners, pair_mask, own, block)


def solution(mesh):
    in_specs = (P("chan", "win"), P(), P())
    out_specs = P(None, None, "win", "chan")
    return jax.shard_map(local, mesh=mesh, in_specs=in_specs, out_specs=out_specs, check_vma=False)
```
